1024 devices in a mesh: rep: 4 (over y), exp: 64 (over z, core), opt: 4 (over x).
Axes of the slice: x: 4, y: 4, z: 32, core: 2. Of those that a mesh axis runs over, the one named last changes fastest.
Arguments:
- grad_out: bfloat16 [65536, 3584], P(('rep', 'exp'), 'opt'), may hold values from -0.119628906 to 0.119628906
- hidden: bfloat16 [65536, 2, 1024], P(('rep', 'exp'), None, 'opt'), may hold values from -6 to 6
- expert_ids: int32 [65536, 2], P(('rep', 'exp')), may hold values from 0 to 63, all different within a row; in each aligned block of 256 rows (0 to 255, 256 to 511, ...) at most 12 rows name the same one
- route_weights: float32 [65536, 2], P(('rep', 'exp')), may hold values from 0.05 to 0.5
- first_moment: float32 [64, 1024, 3584], P('exp', 'rep', 'opt'), may hold values from -0.3 to 0.3
- second_moment: float32 [64, 1024, 3584], P('exp', 'rep', 'opt'), may hold values from 0.001 to 0.03
Outputs:
- adam_step: bfloat16 [64, 1024, 3584], P('exp', 'rep', 'opt')
The draws below stay inside these ranges and needn't reach their ends.
Inputs may be any that keep to these rules, and one draw needn't show every extreme that they name: `expert_ids`: each token names 2 different experts; the 256 tokens of one device name one expert at most 12 times, and some device reaches 12.
All inputs are finite; a program needn't handle non-finite values.
Results may differ from the reference program's by a relative error of at most 0.0075.
Values may be sent and summed in bfloat16 or wider, within the bound.
No kernel may reach another device: no remote copies, remote signals or barrier semaphores. Data moves between devices by JAX's collectives and lax.ppermute only.
A program may use at most 32 MiB of HBM per device.

```python
import math
import jax
import jax.numpy as jnp
import numpy as np
from jax import lax

D = 3584
FW = 1024
TOPW = 2
TOK_DEV = 256
EXPERTS = 64
CAP = 12
TOKENS = 65536
N_REP = 4
N_EXP = 64


def shard_levels(rng, extent, cuts, low, high):
    loudness, own = 1.0, jax.random.fold_in(rng, 6)
    for position, blocks in cuts:
        heights = jnp.exp(jax.random.uniform(jax.random.fold_in(own, position), (blocks,), jnp.float32, low / len(cuts), high / len(cuts)))
        loudness = loudness * jnp.repeat(heights, extent[position] // blocks).reshape([-1 if axis == position else 1 for axis in range(len(extent))])
    return loudness


def assign_block(rng, own, number, rows, count, top, most, slope):
    sequence = jax.random.permutation(rng, count)
    crowded, usual = portions_of(count, rows * top, most, slope, True), portions_of(count, rows * top, most, slope, False)
    places = jnp.arange(count)

    def named(lengths, turn):
        used = int((lengths > 0).sum())
        fixed = max(1, used // 4)
        shifted = fixed + (places - fixed + turn * (used - fixed)) % max(1, count - fixed)
        return jnp.zeros((count,), jnp.int32).at[sequence[jnp.where(places < fixed, places, shifted)]].set(jnp.asarray(lengths, jnp.int32))

    lengths = jnp.where(number % 4 == 0, named(crowded, number // 4), named(usual, number - number // 4 - 1))
    mixed = jax.random.permutation(jax.random.fold_in(own, 3), count)
    source_of, receiver = mixed[0:count // 2 * 2:2], mixed[1:count // 2 * 2:2]
    room = jnp.minimum(lengths[source_of] - 1, most - lengths[receiver]) // 2
    room = jnp.where((source_of == sequence[0]) | (receiver == sequence[0]) | (lengths[receiver] == 0), 0, jnp.maximum(room, 0))
    shifted = jax.random.randint(jax.random.fold_in(own, 4), (count // 2,), 0, 1 << 20) % (room + 1)
    lengths = lengths.at[source_of].add(-shifted).at[receiver].add(shifted)
    members = jnp.searchsorted(jnp.cumsum(lengths), jnp.arange(rows * top), side="right").astype(jnp.int32)
    table = members.reshape(top, rows).T
    table = table[jax.random.permutation(jax.random.fold_in(own, 1), rows)]
    turn = jax.random.randint(jax.random.fold_in(own, 2), (rows, 1), 0, top)
    return jnp.take_along_axis(table, (jnp.arange(top)[None, :] + turn) % top, axis=1)


def portions_of(amount, total, most, lean, full):
    weights = [(1 << 20) // math.isqrt(standing ** lean) + 1 for standing in range(1, amount + 1)]
    largest = most if full else min(most, max(-(-total // amount), total * weights[0] // sum(weights)))
    least = 1 if total - largest >= amount - 1 else 0
    given, surplus = [largest] + [least] * (amount - 1), total - largest - least * (amount - 1)
    while surplus > 0:
        movable = [i for i in range(1, amount) if given[i] < largest] or [i for i in range(1, amount) if given[i] < most]
        mass, budget = sum([weights[i] for i in movable]), surplus
        for i in movable:
            addition = min(most - given[i], max(1, budget * weights[i] // mass), surplus)
            given[i] = given[i] + addition
            surplus = surplus - addition
    return np.array(given)


def gaussian(rng, shape, spread, reach, cuts=(), kind=jnp.bfloat16):
    gain = shard_levels(rng, shape, cuts, -0.22, 0.18) if cuts else 1.0
    drawn = jax.random.normal(rng, shape, jnp.float32) * spread * gain
    return jnp.minimum(jnp.maximum(drawn, -reach), reach).astype(kind)


def setup_inputs(seed: int = 0) -> dict:
    splits = jax.random.split(jax.random.key(seed), 7)
    grad_out = gaussian(splits[0], (TOKENS, D), 0.02, 0.119628906, ((0, 256), (1, 4)))
    hidden = gaussian(splits[1], (TOKENS, TOPW, FW), 1.0, 6.0, ((0, 256), (2, 4)))
    expert_ids_keys = jax.random.split(jax.random.fold_in(splits[2], 1), TOKENS // TOK_DEV)
    expert_ids_turns = jax.random.permutation(jax.random.fold_in(splits[2], 3), TOKENS // TOK_DEV)
    expert_ids = jax.vmap(lambda own, number: assign_block(jax.random.fold_in(splits[2], 2), own, number, TOK_DEV, EXPERTS, TOPW, CAP, 2))(expert_ids_keys, expert_ids_turns).reshape((TOKENS, TOPW))
    route_weights = jnp.clip(0.05 + 0.45 * jax.random.uniform(splits[3], (TOKENS, TOPW), jnp.float32) ** shard_levels(splits[3], (TOKENS, TOPW), ((0, 256),), -0.2, 0.2), 0.05, 0.5)
    first_moment = gaussian(splits[4], (EXPERTS, FW, D), 0.05, 0.3, ((0, 64), (1, 4), (2, 4)), jnp.float32)
    second_moment = jnp.clip(jnp.exp(math.log(0.03) - 3.4011973 * jax.random.uniform(splits[5], (EXPERTS, FW, D), jnp.float32) ** shard_levels(splits[5], (EXPERTS, FW, D), ((0, 64), (1, 4), (2, 4)), -0.2, 0.2)), 0.001, 0.03)
    return {"grad_out": grad_out, "hidden": hidden, "expert_ids": expert_ids, "route_weights": route_weights, "first_moment": first_moment, "second_moment": second_moment}


first_decay = 0.9
second_decay = 0.95
first_bias = 1.0 - 0.9 ** 10
second_bias = 1.0 - 0.95 ** 10
epsilon = 1e-08

def reference(grad_out, hidden, expert_ids, route_weights, first_moment, second_moment):
    assigned = TOKENS * TOPW
    flat_ids = expert_ids.reshape(assigned)
    scaled = (route_weights[:, :, None] * grad_out[:, None, :]).astype(jnp.bfloat16).reshape(assigned, D)
    flat_hidden = hidden.reshape(assigned, FW)
    order = jnp.argsort(flat_ids, stable=True).astype(jnp.int32)
    labels = jnp.arange(EXPERTS, dtype=jnp.int32)
    counts = lax.optimization_barrier(jnp.sum((flat_ids[:, None] == labels[None, :]).astype(jnp.int32), axis=0)).astype(jnp.int32)
    offsets = (jnp.cumsum(counts) - counts).astype(jnp.int32)
    limit = N_REP * N_EXP * CAP
    padded = jnp.concatenate([order, jnp.zeros((limit,), jnp.int32)])

    def one_slot(expert):
        picked = lax.dynamic_slice_in_dim(padded, offsets[expert], limit)
        valid = (jnp.arange(limit, dtype=jnp.int32) < counts[expert]).astype(scaled.dtype)
        rows = scaled[picked] * valid[:, None]
        columns = flat_hidden[picked]
        gradient = jnp.dot(columns.T, rows, preferred_element_type=jnp.float32)
        first_new = first_decay * first_moment[expert] + (1.0 - first_decay) * gradient
        second_new = second_decay * second_moment[expert] + (1.0 - second_decay) * gradient * gradient
        update = first_new / first_bias / (jnp.sqrt(second_new / second_bias) + epsilon)
        return update.astype(jnp.bfloat16)
    return lax.map(one_slot, labels)
```

```python
import functools

import jax
import jax.numpy as jnp
from jax import lax
from jax.experimental import pallas as pl
from jax.experimental.pallas import tpu as pltpu
from jax.sharding import Mesh
from jax.sharding import PartitionSpec as P

first_decay = 0.9
second_decay = 0.95
first_bias = 1.0 - 0.9**10
second_bias = 1.0 - 0.95**10
epsilon = 1e-08

LATE = 256
CAP = 12
PAIR = 2 * CAP
SMEM = pl.BlockSpec(memory_space=pltpu.SMEM)
VMEM = pl.BlockSpec(memory_space=pltpu.VMEM)
ANY = pl.BlockSpec(memory_space=pl.ANY)
PARAMS = pltpu.CompilerParams(vmem_limit_bytes=32 * 1024 * 1024)


def call(kernel, outs, in_specs, *args):
    return pl.pallas_call(
        kernel,
        out_shape=outs,
        in_specs=in_specs,
        out_specs=jax.tree.map(lambda _: VMEM, outs),
        compiler_params=PARAMS,
    )(*args)


def hot(rows, slot):
    columns = slot.shape[1]
    return lax.broadcasted_iota(jnp.int32, (rows, columns), 0) == slot


def ones_of(mask):
    return jnp.where(mask, 1.0, 0.0).astype(jnp.bfloat16)


def expert_slots(meta_ref, mine, owners):
    ids = meta_ref[0:2, :].astype(jnp.int32)
    ids = jnp.concatenate([ids[0:1, :], ids[1:2, :]], axis=1)
    count = ids.shape[1]
    named = jnp.where(hot(owners, ids), 1.0, 0.0)
    before = lax.broadcasted_iota(jnp.int32, (count, count), 0) < lax.broadcasted_iota(
        jnp.int32, (count, count), 1
    )
    earlier = jnp.dot(
        named.astype(jnp.bfloat16), ones_of(before), preferred_element_type=jnp.float32
    )
    place = jnp.sum(earlier * named, axis=0, keepdims=True).astype(jnp.int32)
    return jnp.right_shift(ids, 1), place, jnp.bitwise_and(ids, 1) == mine


def fill_kernel(chips, where_ref, meta_ref, meta_p_ref, grad_ref, grad_p_ref, hid_ref, hid_p_ref, first_ref, second_ref):
    core = where_ref[1]
    tokens, width = hid_ref.shape[1:]
    units, rows, weight = 0.0, 0.0, 0.0
    sources = ((meta_ref, grad_ref, hid_ref), (meta_p_ref, grad_p_ref, hid_p_ref))
    for source, (meta, grad, hid) in enumerate(sources):
        chip, place, kept = expert_slots(meta, core, 2 * chips)
        slot = jnp.where(kept, chip * PAIR + source * CAP + place, -1)
        masks = [hot(chips * PAIR, slot[:, k * tokens : (k + 1) * tokens]) for k in range(2)]
        for k in range(2):
            units += jnp.dot(ones_of(masks[k]), hid[k], preferred_element_type=jnp.float32)
        rows += jnp.dot(
            ones_of(masks[0] | masks[1]), grad[...], preferred_element_type=jnp.float32
        )
        scale = jnp.where(masks[0], meta[2:3, :], 0.0) + jnp.where(masks[1], meta[3:4, :], 0.0)
        weight += jnp.sum(scale, axis=1, keepdims=True)
    scaled = weight * rows
    early = first_ref.shape[2] - width
    first_ref[:, :, :width] = units.reshape(chips, PAIR, width).astype(first_ref.dtype)
    first_ref[:, :, width:] = scaled[:, :early].reshape(chips, PAIR, early).astype(first_ref.dtype)
    second_ref[...] = scaled[:, early:].reshape(second_ref.shape).astype(second_ref.dtype)


def partial_kernel(start, turned, where_ref, own_ref, before_ref, after_ref, across_ref, rows_ref, *refs):
    outs, units = refs[-5:-1] if turned else refs[-2:-1], refs[-1]
    here = where_ref[2]
    rep = where_ref[3] if turned else 0
    slots, width = units.shape[1:]
    for n, ref in enumerate((own_ref, before_ref, across_ref, after_ref)):
        units[jnp.bitwise_and(here - n + 4, 3)] = ref[:, :, :width].reshape(slots, width)
    rows = rows_ref[:, :, start:].reshape(slots, -1)
    for k in range(4):
        part = lax.dot_general(
            units[jnp.bitwise_and(rep + k, 3)],
            rows,
            (((0,), (0,)), ((), ())),
            preferred_element_type=jnp.float32,
        ).astype(jnp.bfloat16)
        if turned:
            outs[k][...] = part
        else:
            outs[0][k] = part


def turn(x, axis, d):
    n = lax.axis_size(axis)
    return lax.ppermute(x, axis, [(i, (i + d) % n) for i in range(n)])


def partials(where, units, rows, start, turned, after=()):
    chips, pair, width = units[1].shape
    slots = chips * pair
    features = rows.shape[2] - start
    if turned:
        outs = [jax.ShapeDtypeStruct((width, features), jnp.bfloat16)] * 4
    else:
        outs = [jax.ShapeDtypeStruct((4, width, features), jnp.bfloat16)]
    return pl.pallas_call(
        functools.partial(partial_kernel, start, turned),
        out_shape=outs,
        in_specs=[SMEM] + [VMEM] * 5 + [ANY] * len(after),
        out_specs=[VMEM] * len(outs),
        scratch_shapes=[pltpu.VMEM((4, slots, width), jnp.bfloat16)],
        compiler_params=PARAMS,
    )(where, *units, rows, *after)


def update(gradient, first_moment, second_moment):
    first_new = first_decay * first_moment + (1.0 - first_decay) * gradient
    second_new = second_decay * second_moment + (1.0 - second_decay) * gradient * gradient
    step = first_new / first_bias / (jnp.sqrt(second_new / second_bias) + epsilon)
    return step.astype(jnp.bfloat16)


def body(grad_out, hidden, expert_ids, route_weights, first_moment, second_moment):
    chips = lax.axis_size("z")
    width, features = hidden.shape[2], grad_out.shape[1]
    early = features - LATE
    where = jnp.stack([lax.axis_index(a) for a in ("z", "core", "opt", "rep")]).astype(jnp.int32)
    meta = jnp.concatenate([expert_ids.T.astype(jnp.float32), route_weights.T], axis=0)
    hid = hidden.transpose(1, 0, 2)
    first, second = call(
        functools.partial(fill_kernel, chips),
        [
            jax.ShapeDtypeStruct((chips, PAIR, width + early), jnp.bfloat16),
            jax.ShapeDtypeStruct((chips, PAIR, features - early), jnp.bfloat16),
        ],
        [SMEM] + [VMEM] * 6,
        where, meta, turn(meta, "core", 1), grad_out, turn(grad_out, "core", 1), hid, turn(hid, "core", 1),
    )
    first = lax.all_to_all(first, "z", split_axis=0, concat_axis=0, tiled=True)
    second = lax.all_to_all(second, "z", split_axis=0, concat_axis=0, tiled=True)
    own = first[:, :, :width]
    units = [first, turn(own, "opt", 1), turn(own, "opt", -1), turn(own, "opt", 2)]
    kept, *sent = partials(where, units, first, width, True)
    came = [turn(part, "rep", k + 1) for k, part in enumerate(sent)]
    gradient = sum((part.astype(jnp.float32) for part in came), kept.astype(jnp.float32))
    steps = [update(gradient, first_moment[0, :, :early], second_moment[0, :, :early])]
    (sent,) = partials(where, units, second, 0, False, came)
    came = lax.all_to_all(sent, "rep", split_axis=0, concat_axis=0, tiled=True)
    gradient = jnp.sum(came.astype(jnp.float32), axis=0)
    steps.append(update(gradient, first_moment[0, :, early:], second_moment[0, :, early:]))
    return jnp.concatenate(steps, axis=1)[None]


def solution(mesh):
    reps, exps, opts = (mesh.shape[a] for a in ("rep", "exp", "opt"))
    split = Mesh(mesh.devices.reshape(reps, exps // 2, 2, opts), ("rep", "z", "core", "opt"))
    exp = ("z", "core")
    tokens = ("rep",) + exp
    placed = (
        P(tokens, "opt"),
        P(tokens, None, "opt"),
        P(tokens, None),
        P(tokens, None),
        P(exp, "rep", "opt"),
        P(exp, "rep", "opt"),
    )
    return jax.shard_map(
        body, mesh=split, in_specs=placed, out_specs=P(exp, "rep", "opt"), check_vma=False
    )
```

```python
import functools

import jax
import jax.numpy as jnp
from jax import lax
from jax.experimental import pallas as pl
from jax.experimental.pallas import tpu as pltpu
from jax.sharding import Mesh
from jax.sharding import PartitionSpec as P

first_decay = 0.9
second_decay = 0.95
first_bias = 1.0 - 0.9**10
second_bias = 1.0 - 0.95**10
epsilon = 1e-08

LATE = 384
CAP = 12
PAIR = 2 * CAP
SMEM = pl.BlockSpec(memory_space=pltpu.SMEM)
VMEM = pl.BlockSpec(memory_space=pltpu.VMEM)
ANY = pl.BlockSpec(memory_space=pl.ANY)
PARAMS = pltpu.CompilerParams(vmem_limit_bytes=32 * 1024 * 1024)


def call(kernel, outs, in_specs, *args):
    return pl.pallas_call(
        kernel,
        out_shape=outs,
        in_specs=in_specs,
        out_specs=jax.tree.map(lambda _: VMEM, outs),
        compiler_params=PARAMS,
    )(*args)


def hot(rows, slot):
    columns = slot.shape[1]
    return lax.broadcasted_iota(jnp.int32, (rows, columns), 0) == slot


def ones_of(mask):
    return jnp.where(mask, 1.0, 0.0).astype(jnp.bfloat16)


def expert_slots(ids, mine, owners):
    ids = ids.astype(jnp.int32)
    ids = jnp.concatenate([ids[0:1, :], ids[1:2, :]], axis=1)
    count = ids.shape[1]
    named = jnp.where(hot(owners, ids), 1.0, 0.0)
    before = lax.broadcasted_iota(jnp.int32, (count, count), 0) < lax.broadcasted_iota(
        jnp.int32, (count, count), 1
    )
    earlier = jnp.dot(
        named.astype(jnp.bfloat16), ones_of(before), preferred_element_type=jnp.float32
    )
    place = jnp.sum(earlier * named, axis=0, keepdims=True).astype(jnp.int32)
    return jnp.right_shift(ids, 1), place, jnp.bitwise_and(ids, 1) == mine


def pack_kernel(ids_ref, weights_ref, hid_ref, out_ref):
    tokens = hid_ref.shape[0]
    rest = weights_ref[...]
    rows = [ids_ref[...].astype(jnp.float32)]
    for _ in range(3):
        part = rest.astype(jnp.bfloat16).astype(jnp.float32)
        rows.append(part)
        rest = rest - part
    rows = jnp.concatenate(rows + [jnp.zeros((8, tokens), jnp.float32)], axis=0)
    for k in range(2):
        out_ref[k, :tokens, :] = hid_ref[:, k, :]
        out_ref[k, tokens:, :] = rows.astype(jnp.bfloat16)


def unpacked(pack_ref):
    tokens = pack_ref.shape[2]
    rows = pack_ref[0, tokens:, :].astype(jnp.float32)
    weights = (rows[2:4] + rows[4:6]) + rows[6:8]
    return rows[0:2], weights, [pack_ref[k, :tokens, :] for k in range(2)]


def fill_kernel(chips, where_ref, grad_ref, grad_p_ref, pack_ref, pack_p_ref, first_ref, second_ref):
    core = where_ref[1]
    tokens, width = grad_ref.shape[0], pack_ref.shape[2]
    units, rows, weight = 0.0, 0.0, 0.0
    for source, (grad, pack) in enumerate(((grad_ref, pack_ref), (grad_p_ref, pack_p_ref))):
        ids, weights, hid = unpacked(pack)
        chip, place, kept = expert_slots(ids, core, 2 * chips)
        slot = jnp.where(kept, chip * PAIR + source * CAP + place, -1)
        masks = [hot(chips * PAIR, slot[:, k * tokens : (k + 1) * tokens]) for k in range(2)]
        for k in range(2):
            units += jnp.dot(ones_of(masks[k]), hid[k], preferred_element_type=jnp.float32)
        rows += jnp.dot(
            ones_of(masks[0] | masks[1]), grad[...], preferred_element_type=jnp.float32
        )
        scale = jnp.where(masks[0], weights[0:1], 0.0) + jnp.where(masks[1], weights[1:2], 0.0)
        weight += jnp.sum(scale, axis=1, keepdims=True)
    scaled = weight * rows
    early = first_ref.shape[2] - width
    first_ref[:, :, :width] = units.reshape(chips, PAIR, width).astype(first_ref.dtype)
    first_ref[:, :, width:] = scaled[:, :early].reshape(chips, PAIR, early).astype(first_ref.dtype)
    second_ref[...] = scaled[:, early:].reshape(second_ref.shape).astype(second_ref.dtype)


def partial_kernel(start, turned, where_ref, own_ref, before_ref, after_ref, across_ref, rows_ref, *refs):
    outs, units = refs[-5:-1] if turned else refs[-2:-1], refs[-1]
    here = where_ref[2]
    rep = where_ref[3] if turned else 0
    slots, width = units.shape[1:]
    for n, ref in enumerate((own_ref, before_ref, across_ref, after_ref)):
        units[jnp.bitwise_and(here - n + 4, 3)] = ref[:, :, :width].reshape(slots, width)
    rows = rows_ref[:, :, start:].reshape(slots, -1)
    for k in range(4):
        part = lax.dot_general(
            units[jnp.bitwise_and(rep + k, 3)],
            rows,
            (((0,), (0,)), ((), ())),
            preferred_element_type=jnp.float32,
        ).astype(jnp.bfloat16)
        if turned:
            outs[k][...] = part
        else:
            outs[0][k] = part


def turn(x, axis, d):
    n = lax.axis_size(axis)
    return lax.ppermute(x, axis, [(i, (i + d) % n) for i in range(n)])


def partials(where, units, rows, start, turned, after=()):
    chips, pair, width = units[1].shape
    slots = chips * pair
    features = rows.shape[2] - start
    if turned:
        outs = [jax.ShapeDtypeStruct((width, features), jnp.bfloat16)] * 4
    else:
        outs = [jax.ShapeDtypeStruct((4, width, features), jnp.bfloat16)]
    return pl.pallas_call(
        functools.partial(partial_kernel, start, turned),
        out_shape=outs,
        in_specs=[SMEM] + [VMEM] * 5 + [ANY] * len(after),
        out_specs=[VMEM] * len(outs),
        scratch_shapes=[pltpu.VMEM((4, slots, width), jnp.bfloat16)],
        compiler_params=PARAMS,
    )(where, *units, rows, *after)


def update(gradient, first_moment, second_moment):
    first_new = first_decay * first_moment + (1.0 - first_decay) * gradient
    second_new = second_decay * second_moment + (1.0 - second_decay) * gradient * gradient
    step = first_new / first_bias / (jnp.sqrt(second_new / second_bias) + epsilon)
    return step.astype(jnp.bfloat16)


def body(grad_out, hidden, expert_ids, route_weights, first_moment, second_moment):
    chips = lax.axis_size("z")
    width, features = hidden.shape[2], grad_out.shape[1]
    early = features - LATE
    where = jnp.stack([lax.axis_index(a) for a in ("z", "core", "opt", "rep")]).astype(jnp.int32)
    grad_p = turn(grad_out, "core", 1)
    tokens = hidden.shape[0]
    pack = call(
        pack_kernel,
        jax.ShapeDtypeStruct((2, tokens + 16, width), jnp.bfloat16),
        [VMEM] * 3,
        expert_ids.T, route_weights.T, hidden,
    )
    first, second = call(
        functools.partial(fill_kernel, chips),
        [
            jax.ShapeDtypeStruct((chips, PAIR, width + early), jnp.bfloat16),
            jax.ShapeDtypeStruct((chips, PAIR, features - early), jnp.bfloat16),
        ],
        [SMEM] + [VMEM] * 4,
        where, grad_out, grad_p, pack, turn(pack, "core", 1),
    )
    first = lax.all_to_all(first, "z", split_axis=0, concat_axis=0, tiled=True)
    second = lax.all_to_all(second, "z", split_axis=0, concat_axis=0, tiled=True)
    own = first[:, :, :width]
    units = [first, turn(own, "opt", 1), turn(own, "opt", -1), turn(own, "opt", 2)]
    kept, *sent = partials(where, units, first, width, True)
    came = [turn(part, "rep", k + 1) for k, part in enumerate(sent)]
    gradient = sum((part.astype(jnp.float32) for part in came), kept.astype(jnp.float32))
    steps = [update(gradient, first_moment[0, :, :early], second_moment[0, :, :early])]
    (sent,) = partials(where, units, second, 0, False, came)
    came = lax.all_to_all(sent, "rep", split_axis=0, concat_axis=0, tiled=True)
    gradient = jnp.sum(came.astype(jnp.float32), axis=0)
    steps.append(update(gradient, first_moment[0, :, early:], second_moment[0, :, early:]))
    return jnp.concatenate(steps, axis=1)[None]


def solution(mesh):
    reps, exps, opts = (mesh.shape[a] for a in ("rep", "exp", "opt"))
    split = Mesh(mesh.devices.reshape(reps, exps // 2, 2, opts), ("rep", "z", "core", "opt"))
    exp = ("z", "core")
    tokens = ("rep",) + exp
    placed = (
        P(tokens, "opt"),
        P(tokens, None, "opt"),
        P(tokens, None),
        P(tokens, None),
        P(exp, "rep", "opt"),
        P(exp, "rep", "opt"),
    )
    return jax.shard_map(
        body, mesh=split, in_specs=placed, out_specs=P(exp, "rep", "opt"), check_vma=False
    )
```

```python
import functools

import jax
import jax.numpy as jnp
from jax import lax
from jax.experimental import pallas as pl
from jax.experimental.pallas import tpu as pltpu
from jax.sharding import Mesh
from jax.sharding import PartitionSpec as P

first_decay = 0.9
second_decay = 0.95
first_bias = 1.0 - 0.9**10
second_bias = 1.0 - 0.95**10
epsilon = 1e-08

LATE = 384
CAP = 12
PAIR = 2 * CAP
SMEM = pl.BlockSpec(memory_space=pltpu.SMEM)
VMEM = pl.BlockSpec(memory_space=pltpu.VMEM)
ANY = pl.BlockSpec(memory_space=pl.ANY)
PARAMS = pltpu.CompilerParams(vmem_limit_bytes=32 * 1024 * 1024)


def call(kernel, outs, in_specs, *args, cost=None):
    return pl.pallas_call(
        kernel,
        cost_estimate=cost,
        out_shape=outs,
        in_specs=in_specs,
        out_specs=jax.tree.map(lambda _: VMEM, outs),
        compiler_params=PARAMS,
    )(*args)


def hot(rows, slot):
    columns = slot.shape[1]
    return lax.broadcasted_iota(jnp.int32, (rows, columns), 0) == slot


def ones_of(mask):
    return jnp.where(mask, 1.0, 0.0).astype(jnp.bfloat16)


def expert_slots(ids, mine, owners):
    ids = ids.astype(jnp.int32)
    ids = jnp.concatenate([ids[0:1, :], ids[1:2, :]], axis=1)
    count = ids.shape[1]
    named = jnp.where(hot(owners, ids), 1.0, 0.0)
    before = lax.broadcasted_iota(jnp.int32, (count, count), 0) < lax.broadcasted_iota(
        jnp.int32, (count, count), 1
    )
    earlier = jnp.dot(
        named.astype(jnp.bfloat16), ones_of(before), preferred_element_type=jnp.float32
    )
    place = jnp.sum(earlier * named, axis=0, keepdims=True).astype(jnp.int32)
    return jnp.right_shift(ids, 1), place, jnp.bitwise_and(ids, 1) == mine


def pack_kernel(ids_ref, weights_ref, hid_ref, out_ref):
    tokens = hid_ref.shape[0]
    rest = weights_ref[...]
    rows = [ids_ref[...].astype(jnp.float32)]
    for _ in range(3):
        part = rest.astype(jnp.bfloat16).astype(jnp.float32)
        rows.append(part)
        rest = rest - part
    rows = jnp.concatenate(rows + [jnp.zeros((8, tokens), jnp.float32)], axis=0)
    for k in range(2):
        out_ref[k, :tokens, :] = hid_ref[:, k, :]
        out_ref[k, tokens:, :] = rows.astype(jnp.bfloat16)


def unpacked(pack_ref):
    tokens = pack_ref.shape[2]
    rows = pack_ref[0, tokens:, :].astype(jnp.float32)
    weights = (rows[2:4] + rows[4:6]) + rows[6:8]
    return rows[0:2], weights, [pack_ref[k, :tokens, :] for k in range(2)]


CHIPS = 32
SHORT = [1, -1, 2, -2, 3, -3, 4]
LONG = [4, -4, 8, -8, 12, -12]
SHORT_SENDS = [[1, 5, 9, 13], [-1, -5, -9, -13], [2, 6, 10, 14], [-2, -6, -10, -14], [3, 7, 11, 15], [-3, -7, -11, -15], [16]]
LONG_SENDS = [[d + (b if d > 0 else -b) for b in range(5 if d == 12 else 4)] for d in LONG]


def fill_kernel(chips, where_ref, grad_ref, grad_p_ref, pack_ref, pack_p_ref, second_ref, *refs):
    *outs, first = refs
    at, core = where_ref[0], where_ref[1]
    tokens, width = grad_ref.shape[0], pack_ref.shape[2]
    units, rows, weight = 0.0, 0.0, 0.0
    for source, (grad, pack) in enumerate(((grad_ref, pack_ref), (grad_p_ref, pack_p_ref))):
        ids, weights, hid = unpacked(pack)
        chip, place, kept = expert_slots(ids, core, 2 * chips)
        slot = jnp.where(kept, chip * PAIR + source * CAP + place, -1)
        masks = [hot(chips * PAIR, slot[:, k * tokens : (k + 1) * tokens]) for k in range(2)]
        for k in range(2):
            units += jnp.dot(ones_of(masks[k]), hid[k], preferred_element_type=jnp.float32)
        rows += jnp.dot(
            ones_of(masks[0] | masks[1]), grad[...], preferred_element_type=jnp.float32
        )
        scale = jnp.where(masks[0], weights[0:1], 0.0) + jnp.where(masks[1], weights[1:2], 0.0)
        weight += jnp.sum(scale, axis=1, keepdims=True)
    scaled = weight * rows
    early = first.shape[2] - width
    first[:, :, :width] = units.reshape(chips, PAIR, width).astype(first.dtype)
    first[:, :, width:] = scaled[:, :early].reshape(chips, PAIR, early).astype(first.dtype)
    second_ref[...] = scaled[:, early:].reshape(second_ref.shape).astype(second_ref.dtype)
    for out, blocks in zip(outs, SHORT_SENDS + [LONG + [0]]):
        for n, d in enumerate(blocks):
            out[n] = first[jnp.bitwise_and(at + d + chips, chips - 1)]


def join_kernel(rest_ref, *refs):
    short, outs = refs[: len(SHORT)], refs[len(SHORT) :]
    for n, (d, blocks) in enumerate(zip(LONG, LONG_SENDS)):
        outs[n][0] = rest_ref[n]
        for b in range(1, len(blocks)):
            step = SHORT.index(blocks[b] - d)
            outs[n][b] = short[step][SHORT_SENDS[step].index(blocks[b])]


def gather_kernel(chips, where_ref, rest_ref, *refs):
    short, far, (units_ref, rows_ref) = refs[: len(SHORT)], refs[len(SHORT) : -2], refs[-2:]
    width = units_ref.shape[2]
    at = where_ref[0] + chips
    blocks = [(0, rest_ref.at[len(LONG)])]
    blocks += [(d, ref.at[0]) for d, ref, sent in zip(SHORT, short, SHORT_SENDS) if sent[0] == d]
    blocks += [(d, ref.at[n]) for ref, sent in zip(far, LONG_SENDS) for n, d in enumerate(sent)]
    for d, block in blocks:
        place = jnp.bitwise_and(at - d, chips - 1)
        units_ref[place] = block[:, :width]
        rows_ref[place] = block[:, width:]


def partial_kernel(start, turned, where_ref, own_ref, before_ref, after_ref, across_ref, rows_ref, *refs):
    outs, units = refs[-5:-1] if turned else refs[-2:-1], refs[-1]
    here = where_ref[2]
    rep = where_ref[3] if turned else 0
    slots, width = units.shape[1:]
    for n, ref in enumerate((own_ref, before_ref, across_ref, after_ref)):
        units[jnp.bitwise_and(here - n + 4, 3)] = ref[:, :, :width].reshape(slots, width)
    rows = rows_ref[:, :, start:].reshape(slots, -1)
    for k in range(4):
        part = lax.dot_general(
            units[jnp.bitwise_and(rep + k, 3)],
            rows,
            (((0,), (0,)), ((), ())),
            preferred_element_type=jnp.float32,
        ).astype(jnp.bfloat16)
        if turned:
            outs[k][...] = part
        else:
            outs[0][k] = part


def turn(x, axis, d):
    n = lax.axis_size(axis)
    return lax.ppermute(x, axis, [(i, (i + d) % n) for i in range(n)])


def partials(where, units, rows, start, turned, after=()):
    chips, pair, width = units[1].shape
    slots = chips * pair
    features = rows.shape[2] - start
    if turned:
        outs = [jax.ShapeDtypeStruct((width, features), jnp.bfloat16)] * 4
    else:
        outs = [jax.ShapeDtypeStruct((4, width, features), jnp.bfloat16)]
    return pl.pallas_call(
        functools.partial(partial_kernel, start, turned),
        out_shape=outs,
        in_specs=[SMEM] + [VMEM] * 5 + [ANY] * len(after),
        out_specs=[VMEM] * len(outs),
        scratch_shapes=[pltpu.VMEM((4, slots, width), jnp.bfloat16)],
        compiler_params=PARAMS,
    )(where, *units, rows, *after)


def update(gradient, first_moment, second_moment):
    first_new = first_decay * first_moment + (1.0 - first_decay) * gradient
    second_new = second_decay * second_moment + (1.0 - second_decay) * gradient * gradient
    step = first_new / first_bias / (jnp.sqrt(second_new / second_bias) + epsilon)
    return step.astype(jnp.bfloat16)


def body(grad_out, hidden, expert_ids, route_weights, first_moment, second_moment):
    chips = lax.axis_size("z")
    width, features = hidden.shape[2], grad_out.shape[1]
    early = features - LATE
    where = jnp.stack([lax.axis_index(a) for a in ("z", "core", "opt", "rep")]).astype(jnp.int32)
    grad_p = turn(grad_out, "core", 1)
    tokens = hidden.shape[0]
    pack = call(
        pack_kernel,
        jax.ShapeDtypeStruct((2, tokens + 16, width), jnp.bfloat16),
        [VMEM] * 3,
        expert_ids.T, route_weights.T, hidden,
    )
    bf16 = jnp.bfloat16

    def blocks(n, columns):
        return jax.ShapeDtypeStruct((n, PAIR, columns), bf16)

    outs = [blocks(chips, features - early)] + [blocks(len(s), width + early) for s in SHORT_SENDS]
    outs += [blocks(len(LONG) + 1, width + early)]
    second, *short, rest = pl.pallas_call(
        functools.partial(fill_kernel, chips),
        out_shape=outs,
        in_specs=[SMEM] + [VMEM] * 4,
        out_specs=[VMEM] * len(outs),
        scratch_shapes=[pltpu.VMEM((chips, PAIR, width + early), bf16)],
        compiler_params=PARAMS,
    )(where, grad_out, grad_p, pack, turn(pack, "core", 1))
    short = [turn(x, "z", d) for x, d in zip(short, SHORT)]
    far = call(
        join_kernel,
        [blocks(len(s), width + early) for s in LONG_SENDS],
        [VMEM] * (1 + len(short)),
        rest, *short,
    )
    far = [turn(x, "z", d) for x, d in zip(far, LONG)]
    second = lax.all_to_all(second, "z", split_axis=0, concat_axis=0, tiled=True)
    units, first = call(
        functools.partial(gather_kernel, chips),
        [blocks(chips, width), blocks(chips, early)],
        [SMEM] + [VMEM] * (1 + len(short) + len(far)),
        where, rest, *short, *far,
        cost=pl.CostEstimate(flops=2000000000000, bytes_accessed=0, transcendentals=0),
    )
    units = [units, turn(units, "opt", 1), turn(units, "opt", -1), turn(units, "opt", 2)]
    kept, *sent = partials(where, units, first, 0, True)
    came = [turn(part, "rep", k + 1) for k, part in enumerate(sent)]
    gradient = sum((part.astype(jnp.float32) for part in came), kept.astype(jnp.float32))
    steps = [update(gradient, first_moment[0, :, :early], second_moment[0, :, :early])]
    (sent,) = partials(where, units, second, 0, False, came)
    came = lax.all_to_all(sent, "rep", split_axis=0, concat_axis=0, tiled=True)
    gradient = jnp.sum(came.astype(jnp.float32), axis=0)
    steps.append(update(gradient, first_moment[0, :, early:], second_moment[0, :, early:]))
    return jnp.concatenate(steps, axis=1)[None]


def solution(mesh):
    reps, exps, opts = (mesh.shape[a] for a in ("rep", "exp", "opt"))
    split = Mesh(mesh.devices.reshape(reps, exps // 2, 2, opts), ("rep", "z", "core", "opt"))
    exp = ("z", "core")
    tokens = ("rep",) + exp
    placed = (
        P(tokens, "opt"),
        P(tokens, None, "opt"),
        P(tokens, None),
        P(tokens, None),
        P(exp, "rep", "opt"),
        P(exp, "rep", "opt"),
    )
    return jax.shard_map(
        body, mesh=split, in_specs=placed, out_specs=P(exp, "rep", "opt"), check_vma=False
    )
```

```python
import functools

import jax
import jax.numpy as jnp
from jax import lax
from jax.experimental import pallas as pl
from jax.experimental.pallas import tpu as pltpu
from jax.sharding import Mesh
from jax.sharding import PartitionSpec as P

first_decay = 0.9
second_decay = 0.95
first_bias = 1.0 - 0.9**10
second_bias = 1.0 - 0.95**10
epsilon = 1e-08

LATE = 384
CAP = 12
PAIR = 2 * CAP
SMEM = pl.BlockSpec(memory_space=pltpu.SMEM)
VMEM = pl.BlockSpec(memory_space=pltpu.VMEM)
ANY = pl.BlockSpec(memory_space=pl.ANY)
PARAMS = pltpu.CompilerParams(vmem_limit_bytes=32 * 1024 * 1024)


def call(kernel, outs, in_specs, *args, cost=None):
    return pl.pallas_call(
        kernel,
        cost_estimate=cost,
        out_shape=outs,
        in_specs=in_specs,
        out_specs=jax.tree.map(lambda _: VMEM, outs),
        compiler_params=PARAMS,
    )(*args)


def hot(rows, slot):
    columns = slot.shape[1]
    return lax.broadcasted_iota(jnp.int32, (rows, columns), 0) == slot


def ones_of(mask):
    return jnp.where(mask, 1.0, 0.0).astype(jnp.bfloat16)


def expert_slots(ids, mine, owners):
    ids = ids.astype(jnp.int32)
    ids = jnp.concatenate([ids[0:1, :], ids[1:2, :]], axis=1)
    count = ids.shape[1]
    named = jnp.where(hot(owners, ids), 1.0, 0.0)
    before = lax.broadcasted_iota(jnp.int32, (count, count), 0) < lax.broadcasted_iota(
        jnp.int32, (count, count), 1
    )
    earlier = jnp.dot(
        named.astype(jnp.bfloat16), ones_of(before), preferred_element_type=jnp.float32
    )
    place = jnp.sum(earlier * named, axis=0, keepdims=True).astype(jnp.int32)
    return jnp.right_shift(ids, 1), place, jnp.bitwise_and(ids, 1) == mine


def pack_kernel(ids_ref, weights_ref, hid_ref, out_ref):
    tokens = hid_ref.shape[0]
    rest = weights_ref[...]
    rows = [ids_ref[...].astype(jnp.float32)]
    for _ in range(3):
        part = rest.astype(jnp.bfloat16).astype(jnp.float32)
        rows.append(part)
        rest = rest - part
    rows = jnp.concatenate(rows + [jnp.zeros((8, tokens), jnp.float32)], axis=0)
    for k in range(2):
        out_ref[k, :tokens, :] = hid_ref[:, k, :]
        out_ref[k, tokens:, :] = rows.astype(jnp.bfloat16)


def unpacked(pack_ref):
    tokens = pack_ref.shape[2]
    rows = pack_ref[0, tokens:, :].astype(jnp.float32)
    weights = (rows[2:4] + rows[4:6]) + rows[6:8]
    return rows[0:2], weights, [pack_ref[k, :tokens, :] for k in range(2)]


CHIPS = 32
SHORT = [1, -1, 2, -2, 3, -3, 4]
LONG = [-4, -12, 8, -8, 12, 4]
SHORT_SENDS = [[1, 5, 9, 13], [-1, -5, -9, -13], [2, 6, 10, 14], [-2, -6, -10, -14], [3, 7, 11, 15], [-3, -7, -11, -15], [16]]
LONG_SENDS = [[d + (b if d > 0 else -b) for b in range(5 if d == 12 else 4)] for d in LONG]


def fill_kernel(chips, where_ref, grad_ref, grad_p_ref, pack_ref, pack_p_ref, second_ref, *refs):
    *outs, first = refs
    at, core = where_ref[0], where_ref[1]
    tokens, width = grad_ref.shape[0], pack_ref.shape[2]
    units, rows, weight = 0.0, 0.0, 0.0
    for source, (grad, pack) in enumerate(((grad_ref, pack_ref), (grad_p_ref, pack_p_ref))):
        ids, weights, hid = unpacked(pack)
        chip, place, kept = expert_slots(ids, core, 2 * chips)
        slot = jnp.where(kept, chip * PAIR + source * CAP + place, -1)
        masks = [hot(chips * PAIR, slot[:, k * tokens : (k + 1) * tokens]) for k in range(2)]
        for k in range(2):
            units += jnp.dot(ones_of(masks[k]), hid[k], preferred_element_type=jnp.float32)
        rows += jnp.dot(
            ones_of(masks[0] | masks[1]), grad[...], preferred_element_type=jnp.float32
        )
        scale = jnp.where(masks[0], weights[0:1], 0.0) + jnp.where(masks[1], weights[1:2], 0.0)
        weight += jnp.sum(scale, axis=1, keepdims=True)
    scaled = weight * rows
    early = first.shape[2] - width
    first[:, :, :width] = units.reshape(chips, PAIR, width).astype(first.dtype)
    first[:, :, width:] = scaled[:, :early].reshape(chips, PAIR, early).astype(first.dtype)
    second_ref[...] = scaled[:, early:].reshape(second_ref.shape).astype(second_ref.dtype)
    for out, blocks in zip(outs, SHORT_SENDS + [LONG + [0]]):
        for n, d in enumerate(blocks):
            out[n] = first[jnp.bitwise_and(at + d + chips, chips - 1)]


def join_kernel(rest_ref, *refs):
    short, outs = refs[: len(SHORT)], refs[len(SHORT) :]
    for n, (d, blocks) in enumerate(zip(LONG, LONG_SENDS)):
        outs[n][0] = rest_ref[n]
        for b in range(1, len(blocks)):
            step = SHORT.index(blocks[b] - d)
            outs[n][b] = short[step][SHORT_SENDS[step].index(blocks[b])]


def gather_kernel(chips, where_ref, rest_ref, *refs):
    short, far, (units_ref, rows_ref) = refs[: len(SHORT)], refs[len(SHORT) : -2], refs[-2:]
    width = units_ref.shape[2]
    at = where_ref[0] + chips
    blocks = [(0, rest_ref.at[len(LONG)])]
    blocks += [(d, ref.at[0]) for d, ref, sent in zip(SHORT, short, SHORT_SENDS) if sent[0] == d]
    blocks += [(d, ref.at[n]) for ref, sent in zip(far, LONG_SENDS) for n, d in enumerate(sent)]
    for d, block in blocks:
        place = jnp.bitwise_and(at - d, chips - 1)
        units_ref[place] = block[:, :width]
        rows_ref[place] = block[:, width:]


def first_kernel(where_ref, own_ref, before_ref, after_ref, across_ref, rows_ref, *refs):
    *outs, units = refs
    here, rep = where_ref[2], where_ref[3]
    slots = units.shape[2]
    for n, ref in enumerate((own_ref, before_ref, across_ref, after_ref)):
        units[jnp.bitwise_and(here - n + 4, 3)] = ref[...].reshape(slots, -1).T
    rows = rows_ref[...].reshape(slots, -1)
    for k, out in enumerate(outs):
        part = jnp.dot(units[jnp.bitwise_and(rep + k, 3)], rows, preferred_element_type=jnp.float32)
        out[...] = part.astype(out.dtype)


def second_kernel(units_ref, rows_ref, *refs):
    out_ref = refs[-1]
    rows = rows_ref[...].reshape(units_ref.shape[2], -1)
    for k in range(4):
        part = jnp.dot(units_ref[k], rows, preferred_element_type=jnp.float32)
        out_ref[k] = part.astype(out_ref.dtype)


def turn(x, axis, d):
    n = lax.axis_size(axis)
    return lax.ppermute(x, axis, [(i, (i + d) % n) for i in range(n)])


def update(gradient, first_moment, second_moment):
    first_new = first_decay * first_moment + (1.0 - first_decay) * gradient
    second_new = second_decay * second_moment + (1.0 - second_decay) * gradient * gradient
    step = first_new / first_bias / (jnp.sqrt(second_new / second_bias) + epsilon)
    return step.astype(jnp.bfloat16)


def body(grad_out, hidden, expert_ids, route_weights, first_moment, second_moment):
    chips = lax.axis_size("z")
    width, features = hidden.shape[2], grad_out.shape[1]
    early = features - LATE
    where = jnp.stack([lax.axis_index(a) for a in ("z", "core", "opt", "rep")]).astype(jnp.int32)
    grad_p = turn(grad_out, "core", 1)
    tokens = hidden.shape[0]
    pack = call(
        pack_kernel,
        jax.ShapeDtypeStruct((2, tokens + 16, width), jnp.bfloat16),
        [pl.BlockSpec()] * 3,
        expert_ids.T, route_weights.T, hidden,
    )
    bf16 = jnp.bfloat16

    def blocks(n, columns):
        return jax.ShapeDtypeStruct((n, PAIR, columns), bf16)

    outs = [blocks(chips, features - early)] + [blocks(len(s), width + early) for s in SHORT_SENDS]
    outs += [blocks(len(LONG) + 1, width + early)]
    second, *short, rest = pl.pallas_call(
        functools.partial(fill_kernel, chips),
        out_shape=outs,
        in_specs=[SMEM] + [VMEM] * 4,
        out_specs=[VMEM] * len(outs),
        scratch_shapes=[pltpu.VMEM((chips, PAIR, width + early), bf16)],
        compiler_params=PARAMS,
    )(where, grad_out, grad_p, pack, turn(pack, "core", 1))
    short = [turn(x, "z", d) for x, d in zip(short, SHORT)]
    far = call(
        join_kernel,
        [blocks(len(s), width + early) for s in LONG_SENDS],
        [VMEM] * (1 + len(short)),
        rest, *short,
    )
    far = [turn(x, "z", d) for x, d in zip(far, LONG)]
    second = lax.all_to_all(second, "z", split_axis=0, concat_axis=0, tiled=True)
    units, first = call(
        functools.partial(gather_kernel, chips),
        [blocks(chips, width), blocks(chips, early)],
        [SMEM] + [VMEM] * (1 + len(short) + len(far)),
        where, rest, *short, *far,
        cost=pl.CostEstimate(flops=2000000000000, bytes_accessed=0, transcendentals=0),
    )
    units = [units, turn(units, "opt", 1), turn(units, "opt", -1), turn(units, "opt", 2)]
    shape = (width, chips * PAIR)
    kept, *sent, units = call(
        first_kernel,
        [jax.ShapeDtypeStruct((width, early), bf16)] * 4 + [jax.ShapeDtypeStruct((4,) + shape, bf16)],
        [SMEM] + [VMEM] * 5,
        where, *units, first,
    )
    came = [turn(part, "rep", k + 1) for k, part in enumerate(sent)]
    gradient = sum((part.astype(jnp.float32) for part in came), kept.astype(jnp.float32))
    steps = [update(gradient, first_moment[0, :, :early], second_moment[0, :, :early])]
    sent = call(
        second_kernel,
        jax.ShapeDtypeStruct((4, width, features - early), bf16),
        [VMEM] * 2 + [ANY] * len(came),
        units, second, *came,
    )
    came = lax.all_to_all(sent, "rep", split_axis=0, concat_axis=0, tiled=True)
    gradient = jnp.sum(came.astype(jnp.float32), axis=0)
    steps.append(update(gradient, first_moment[0, :, early:], second_moment[0, :, early:]))
    return jnp.concatenate(steps, axis=1)[None]


def solution(mesh):
    reps, exps, opts = (mesh.shape[a] for a in ("rep", "exp", "opt"))
    split = Mesh(mesh.devices.reshape(reps, exps // 2, 2, opts), ("rep", "z", "core", "opt"))
    exp = ("z", "core")
    tokens = ("rep",) + exp
    placed = (
        P(tokens, "opt"),
        P(tokens, None, "opt"),
        P(tokens, None),
        P(tokens, None),
        P(exp, "rep", "opt"),
        P(exp, "rep", "opt"),
    )
    return jax.shard_map(
        body, mesh=split, in_specs=placed, out_specs=P(exp, "rep", "opt"), check_vma=False
    )
```

```python
import functools

import jax
import jax.numpy as jnp
from jax import lax
from jax.experimental import pallas as pl
from jax.experimental.pallas import tpu as pltpu
from jax.sharding import Mesh
from jax.sharding import PartitionSpec as P

first_decay = 0.9
second_decay = 0.95
first_bias = 1.0 - 0.9**10
second_bias = 1.0 - 0.95**10
epsilon = 1e-08

LATE = 384
CAP = 12
PAIR = 2 * CAP
SMEM = pl.BlockSpec(memory_space=pltpu.SMEM)
VMEM = pl.BlockSpec(memory_space=pltpu.VMEM)
ANY = pl.BlockSpec(memory_space=pl.ANY)
PARAMS = pltpu.CompilerParams(vmem_limit_bytes=32 * 1024 * 1024)


def call(kernel, outs, in_specs, *args, cost=None):
    return pl.pallas_call(
        kernel,
        cost_estimate=cost,
        out_shape=outs,
        in_specs=in_specs,
        out_specs=jax.tree.map(lambda _: VMEM, outs),
        compiler_params=PARAMS,
    )(*args)


def hot(rows, slot):
    columns = slot.shape[1]
    return lax.broadcasted_iota(jnp.int32, (rows, columns), 0) == slot


def ones_of(mask):
    return jnp.where(mask, 1.0, 0.0).astype(jnp.bfloat16)


def expert_slots(ids, mine, owners):
    ids = ids.astype(jnp.int32)
    ids = jnp.concatenate([ids[0:1, :], ids[1:2, :]], axis=1)
    count = ids.shape[1]
    named = jnp.where(hot(owners, ids), 1.0, 0.0)
    before = lax.broadcasted_iota(jnp.int32, (count, count), 0) < lax.broadcasted_iota(
        jnp.int32, (count, count), 1
    )
    earlier = jnp.dot(
        named.astype(jnp.bfloat16), ones_of(before), preferred_element_type=jnp.float32
    )
    place = jnp.sum(earlier * named, axis=0, keepdims=True).astype(jnp.int32)
    return jnp.right_shift(ids, 1), place, jnp.bitwise_and(ids, 1) == mine


def pack_kernel(ids_ref, weights_ref, hid_ref, out_ref):
    tokens = hid_ref.shape[0]
    rest = weights_ref[...]
    rows = [ids_ref[...].astype(jnp.float32)]
    for _ in range(3):
        part = rest.astype(jnp.bfloat16).astype(jnp.float32)
        rows.append(part)
        rest = rest - part
    rows = jnp.concatenate(rows + [jnp.zeros((8, tokens), jnp.float32)], axis=0)
    for k in range(2):
        out_ref[k, :tokens, :] = hid_ref[:, k, :]
        out_ref[k, tokens:, :] = rows.astype(jnp.bfloat16)


def unpacked(pack_ref):
    tokens = pack_ref.shape[2]
    rows = pack_ref[0, tokens:, :].astype(jnp.float32)
    weights = (rows[2:4] + rows[4:6]) + rows[6:8]
    return rows[0:2], weights, [pack_ref[k, :tokens, :] for k in range(2)]


CHIPS = 32
SHORT = [3, -3, 2, -2, 1, -1, 4]
LONG = [-4, -12, 8, -8, 12, 4]
SHORT_SENDS = [[3, 7, 11, 15], [-3, -7, -11, -15], [2, 6, 10, 14], [-2, -6, -10, -14], [1, 5, 9, 13], [-1, -5, -9, -13], [16]]
LONG_SENDS = [[d + (b if d > 0 else -b) for b in range(5 if d == 12 else 4)] for d in LONG]


def fill_kernel(chips, where_ref, grad_ref, grad_p_ref, pack_ref, pack_p_ref, second_ref, *refs):
    *outs, first = refs
    at, core = where_ref[0], where_ref[1]
    tokens, width = grad_ref.shape[0], pack_ref.shape[2]
    units, rows, weight = 0.0, 0.0, 0.0
    for source, (grad, pack) in enumerate(((grad_ref, pack_ref), (grad_p_ref, pack_p_ref))):
        ids, weights, hid = unpacked(pack)
        chip, place, kept = expert_slots(ids, core, 2 * chips)
        slot = jnp.where(kept, chip * PAIR + source * CAP + place, -1)
        masks = [hot(chips * PAIR, slot[:, k * tokens : (k + 1) * tokens]) for k in range(2)]
        for k in range(2):
            units += jnp.dot(ones_of(masks[k]), hid[k], preferred_element_type=jnp.float32)
        rows += jnp.dot(
            ones_of(masks[0] | masks[1]), grad[...], preferred_element_type=jnp.float32
        )
        scale = jnp.where(masks[0], weights[0:1], 0.0) + jnp.where(masks[1], weights[1:2], 0.0)
        weight += jnp.sum(scale, axis=1, keepdims=True)
    scaled = weight * rows
    early = first.shape[2] - width
    first[:, :, :width] = units.reshape(chips, PAIR, width).astype(first.dtype)
    first[:, :, width:] = scaled[:, :early].reshape(chips, PAIR, early).astype(first.dtype)
    second_ref[...] = scaled[:, early:].reshape(second_ref.shape).astype(second_ref.dtype)
    for out, blocks in zip(outs, SHORT_SENDS + [LONG + [0]]):
        for n, d in enumerate(blocks):
            out[n] = first[jnp.bitwise_and(at + d + chips, chips - 1)]


def join_kernel(rest_ref, *refs):
    short, outs = refs[: len(SHORT)], refs[len(SHORT) :]
    for n, (d, blocks) in enumerate(zip(LONG, LONG_SENDS)):
        outs[n][0] = rest_ref[n]
        for b in range(1, len(blocks)):
            step = SHORT.index(blocks[b] - d)
            outs[n][b] = short[step][SHORT_SENDS[step].index(blocks[b])]


def gather_kernel(chips, where_ref, rest_ref, *refs):
    short, far, (units_ref, rows_ref) = refs[: len(SHORT)], refs[len(SHORT) : -2], refs[-2:]
    width = units_ref.shape[2]
    at = where_ref[0] + chips
    blocks = [(0, rest_ref.at[len(LONG)])]
    blocks += [(d, ref.at[0]) for d, ref, sent in zip(SHORT, short, SHORT_SENDS) if sent[0] == d]
    blocks += [(d, ref.at[n]) for ref, sent in zip(far, LONG_SENDS) for n, d in enumerate(sent)]
    for d, block in blocks:
        place = jnp.bitwise_and(at - d, chips - 1)
        units_ref[place] = block[:, :width]
        rows_ref[place] = block[:, width:]


def first_kernel(where_ref, own_ref, before_ref, after_ref, across_ref, rows_ref, *refs):
    *outs, units = refs
    here, rep = where_ref[2], where_ref[3]
    slots = units.shape[2]
    for n, ref in enumerate((own_ref, before_ref, across_ref, after_ref)):
        units[jnp.bitwise_and(here - n + 4, 3)] = ref[...].reshape(slots, -1).T
    rows = rows_ref[...].reshape(slots, -1)
    for k, out in enumerate(outs):
        part = jnp.dot(units[jnp.bitwise_and(rep + k, 3)], rows, preferred_element_type=jnp.float32)
        out[...] = part.astype(out.dtype)


def second_kernel(units_ref, rows_ref, *refs):
    out_ref = refs[-1]
    rows = rows_ref[...].reshape(units_ref.shape[2], -1)
    for k in range(4):
        part = jnp.dot(units_ref[k], rows, preferred_element_type=jnp.float32)
        out_ref[k] = part.astype(out_ref.dtype)


def turn(x, axis, d):
    n = lax.axis_size(axis)
    return lax.ppermute(x, axis, [(i, (i + d) % n) for i in range(n)])


def update(gradient, first_moment, second_moment):
    first_new = first_decay * first_moment + (1.0 - first_decay) * gradient
    second_new = second_decay * second_moment + (1.0 - second_decay) * gradient * gradient
    step = first_new / first_bias / (jnp.sqrt(second_new / second_bias) + epsilon)
    return step.astype(jnp.bfloat16)


def body(grad_out, hidden, expert_ids, route_weights, first_moment, second_moment):
    chips = lax.axis_size("z")
    width, features = hidden.shape[2], grad_out.shape[1]
    early = features - LATE
    where = jnp.stack([lax.axis_index(a) for a in ("z", "core", "opt", "rep")]).astype(jnp.int32)
    grad_p = turn(grad_out, "core", 1)
    tokens = hidden.shape[0]
    pack = call(
        pack_kernel,
        jax.ShapeDtypeStruct((2, tokens + 16, width), jnp.bfloat16),
        [pl.BlockSpec()] * 3,
        expert_ids.T, route_weights.T, hidden,
    )
    bf16 = jnp.bfloat16

    def blocks(n, columns):
        return jax.ShapeDtypeStruct((n, PAIR, columns), bf16)

    outs = [blocks(chips, features - early)] + [blocks(len(s), width + early) for s in SHORT_SENDS]
    outs += [blocks(len(LONG) + 1, width + early)]
    second, *short, rest = pl.pallas_call(
        functools.partial(fill_kernel, chips),
        out_shape=outs,
        in_specs=[SMEM] + [VMEM] * 4,
        out_specs=[VMEM] * len(outs),
        scratch_shapes=[pltpu.VMEM((chips, PAIR, width + early), bf16)],
        compiler_params=PARAMS,
    )(where, grad_out, grad_p, pack, turn(pack, "core", 1))
    short = [turn(x, "z", d) for x, d in zip(short, SHORT)]
    far = call(
        join_kernel,
        [blocks(len(s), width + early) for s in LONG_SENDS],
        [VMEM] * (1 + len(short)),
        rest, *short,
    )
    far = [turn(x, "z", d) for x, d in zip(far, LONG)]
    second = lax.all_to_all(second, "z", split_axis=0, concat_axis=0, tiled=True)
    units, first = call(
        functools.partial(gather_kernel, chips),
        [blocks(chips, width), blocks(chips, early)],
        [SMEM] + [VMEM] * (1 + len(short) + len(far)),
        where, rest, *short, *far,
        cost=pl.CostEstimate(flops=2000000000000, bytes_accessed=0, transcendentals=0),
    )
    units = [units, turn(units, "opt", 1), turn(units, "opt", -1), turn(units, "opt", 2)]
    shape = (width, chips * PAIR)
    kept, *sent, units = call(
        first_kernel,
        [jax.ShapeDtypeStruct((width, early), bf16)] * 4 + [jax.ShapeDtypeStruct((4,) + shape, bf16)],
        [SMEM] + [VMEM] * 5,
        where, *units, first,
    )
    came = [turn(part, "rep", k + 1) for k, part in enumerate(sent)]
    gradient = sum((part.astype(jnp.float32) for part in came), kept.astype(jnp.float32))
    steps = [update(gradient, first_moment[0, :, :early], second_moment[0, :, :early])]
    sent = call(
        second_kernel,
        jax.ShapeDtypeStruct((4, width, features - early), bf16),
        [VMEM] * 2 + [ANY] * len(came),
        units, second, *came,
    )
    came = lax.all_to_all(sent, "rep", split_axis=0, concat_axis=0, tiled=True)
    gradient = jnp.sum(came.astype(jnp.float32), axis=0)
    steps.append(update(gradient, first_moment[0, :, early:], second_moment[0, :, early:]))
    return jnp.concatenate(steps, axis=1)[None]


def solution(mesh):
    reps, exps, opts = (mesh.shape[a] for a in ("rep", "exp", "opt"))
    split = Mesh(mesh.devices.reshape(reps, exps // 2, 2, opts), ("rep", "z", "core", "opt"))
    exp = ("z", "core")
    tokens = ("rep",) + exp
    placed = (
        P(tokens, "opt"),
        P(tokens, None, "opt"),
        P(tokens, None),
        P(tokens, None),
        P(exp, "rep", "opt"),
        P(exp, "rep", "opt"),
    )
    return jax.shard_map(
        body, mesh=split, in_specs=placed, out_specs=P(exp, "rep", "opt"), check_vma=False
    )
```

```python
import functools

import jax
import jax.numpy as jnp
from jax import lax
from jax.experimental import pallas as pl
from jax.experimental.pallas import tpu as pltpu
from jax.sharding import Mesh
from jax.sharding import PartitionSpec as P

first_decay = 0.9
second_decay = 0.95
first_bias = 1.0 - 0.9**10
second_bias = 1.0 - 0.95**10
epsilon = 1e-08

LATE = 384
CAP = 12
PAIR = 2 * CAP
SMEM = pl.BlockSpec(memory_space=pltpu.SMEM)
VMEM = pl.BlockSpec(memory_space=pltpu.VMEM)
ANY = pl.BlockSpec(memory_space=pl.ANY)
PARAMS = pltpu.CompilerParams(vmem_limit_bytes=32 * 1024 * 1024)


def call(kernel, outs, in_specs, *args, cost=None):
    return pl.pallas_call(
        kernel,
        cost_estimate=cost,
        out_shape=outs,
        in_specs=in_specs,
        out_specs=jax.tree.map(lambda _: VMEM, outs),
        compiler_params=PARAMS,
    )(*args)


def hot(rows, slot):
    columns = slot.shape[1]
    return lax.broadcasted_iota(jnp.int32, (rows, columns), 0) == slot


def ones_of(mask):
    return jnp.where(mask, 1.0, 0.0).astype(jnp.bfloat16)


def expert_slots(ids, mine, owners):
    ids = ids.astype(jnp.int32)
    ids = jnp.concatenate([ids[0:1, :], ids[1:2, :]], axis=1)
    count = ids.shape[1]
    named = jnp.where(hot(owners, ids), 1.0, 0.0)
    before = lax.broadcasted_iota(jnp.int32, (count, count), 0) < lax.broadcasted_iota(
        jnp.int32, (count, count), 1
    )
    earlier = jnp.dot(
        named.astype(jnp.bfloat16), ones_of(before), preferred_element_type=jnp.float32
    )
    place = jnp.sum(earlier * named, axis=0, keepdims=True).astype(jnp.int32)
    return jnp.right_shift(ids, 1), place, jnp.bitwise_and(ids, 1) == mine


def pack_kernel(ids_ref, weights_ref, hid_ref, out_ref):
    tokens = hid_ref.shape[0]
    rest = weights_ref[...]
    rows = [ids_ref[...].astype(jnp.float32)]
    for _ in range(3):
        part = rest.astype(jnp.bfloat16).astype(jnp.float32)
        rows.append(part)
        rest = rest - part
    rows = jnp.concatenate(rows + [jnp.zeros((8, tokens), jnp.float32)], axis=0)
    for k in range(2):
        out_ref[k, :tokens, :] = hid_ref[:, k, :]
        out_ref[k, tokens:, :] = rows.astype(jnp.bfloat16)


def unpacked(pack_ref):
    tokens = pack_ref.shape[2]
    rows = pack_ref[0, tokens:, :].astype(jnp.float32)
    weights = (rows[2:4] + rows[4:6]) + rows[6:8]
    return rows[0:2], weights, [pack_ref[k, :tokens, :] for k in range(2)]


CHIPS = 32
SHORT = [3, -3, 2, -2, 1, -1, 4]
LONG = [-4, -12, 8, -8, 12, 4]
SHORT_SENDS = [[3, 7, 11, 15], [-3, -7, -11, -15], [2, 6, 10, 14], [-2, -6, -10, -14], [1, 5, 9, 13], [-1, -5, -9, -13], [16]]
LONG_SENDS = [[d + (b if d > 0 else -b) for b in range(5 if d == 12 else 4)] for d in LONG]


def fill_kernel(chips, where_ref, grad_ref, grad_p_ref, pack_ref, pack_p_ref, second_ref, *refs):
    *outs, first = refs
    at, core = where_ref[0], where_ref[1]
    tokens, width = grad_ref.shape[0], pack_ref.shape[2]
    units, rows, weight = 0.0, 0.0, 0.0
    for source, (grad, pack) in enumerate(((grad_ref, pack_ref), (grad_p_ref, pack_p_ref))):
        ids, weights, hid = unpacked(pack)
        chip, place, kept = expert_slots(ids, core, 2 * chips)
        slot = jnp.where(kept, chip * PAIR + source * CAP + place, -1)
        masks = [hot(chips * PAIR, slot[:, k * tokens : (k + 1) * tokens]) for k in range(2)]
        for k in range(2):
            units += jnp.dot(ones_of(masks[k]), hid[k], preferred_element_type=jnp.float32)
        rows += jnp.dot(
            ones_of(masks[0] | masks[1]), grad[...], preferred_element_type=jnp.float32
        )
        scale = jnp.where(masks[0], weights[0:1], 0.0) + jnp.where(masks[1], weights[1:2], 0.0)
        weight += jnp.sum(scale, axis=1, keepdims=True)
    scaled = weight * rows
    early = first.shape[2] - width
    first[:, :, :width] = units.reshape(chips, PAIR, width).astype(first.dtype)
    first[:, :, width:] = scaled[:, :early].reshape(chips, PAIR, early).astype(first.dtype)
    second_ref[...] = scaled[:, early:].reshape(second_ref.shape).astype(second_ref.dtype)
    for out, blocks in zip(outs, SHORT_SENDS + [LONG + [0]]):
        for n, d in enumerate(blocks):
            out[n] = first[jnp.bitwise_and(at + d + chips, chips - 1)]


def join_kernel(rest_ref, *refs):
    short, outs = refs[: len(SHORT)], refs[len(SHORT) :]
    for n, (d, blocks) in enumerate(zip(LONG, LONG_SENDS)):
        outs[n][0] = rest_ref[n]
        for b in range(1, len(blocks)):
            step = SHORT.index(blocks[b] - d)
            outs[n][b] = short[step][SHORT_SENDS[step].index(blocks[b])]


def gather_kernel(chips, where_ref, rest_ref, *refs):
    short, far, (units_ref, rows_ref) = refs[: len(SHORT)], refs[len(SHORT) : -2], refs[-2:]
    width = units_ref.shape[2]
    at = where_ref[0] + chips
    blocks = [(0, rest_ref.at[len(LONG)])]
    blocks += [(d, ref.at[0]) for d, ref, sent in zip(SHORT, short, SHORT_SENDS) if sent[0] == d]
    blocks += [(d, ref.at[n]) for ref, sent in zip(far, LONG_SENDS) for n, d in enumerate(sent)]
    for d, block in blocks:
        place = jnp.bitwise_and(at - d, chips - 1)
        units_ref[place] = block[:, :width]
        rows_ref[place] = block[:, width:]


def first_kernel(where_ref, own_ref, before_ref, after_ref, across_ref, rows_ref, *refs):
    *outs, units = refs
    here, rep = where_ref[2], where_ref[3]
    slots = units.shape[2]
    for n, ref in enumerate((own_ref, before_ref, across_ref, after_ref)):
        units[jnp.bitwise_and(here - n + 4, 3)] = ref[...].reshape(slots, -1).T
    rows = rows_ref[...].reshape(slots, -1)
    for k, out in enumerate(outs):
        part = jnp.dot(units[jnp.bitwise_and(rep + k, 3)], rows, preferred_element_type=jnp.float32)
        out[...] = part.astype(out.dtype)


def second_kernel(units_ref, rows_ref, *refs):
    out_ref = refs[-1]
    rows = rows_ref[...].reshape(units_ref.shape[2], -1)
    for k in range(4):
        part = jnp.dot(units_ref[k], rows, preferred_element_type=jnp.float32)
        out_ref[k] = part.astype(out_ref.dtype)


def turn(x, axis, d):
    n = lax.axis_size(axis)
    return lax.ppermute(x, axis, [(i, (i + d) % n) for i in range(n)])


def update(gradient, first_moment, second_moment):
    first_new = first_decay * first_moment + (1.0 - first_decay) * gradient
    second_new = second_decay * second_moment + (1.0 - second_decay) * gradient * gradient
    step = first_new / first_bias / (jnp.sqrt(second_new / second_bias) + epsilon)
    return step.astype(jnp.bfloat16)


def finish_kernel(step_ref, came_ref, first_ref, second_ref, out_ref):
    early = step_ref.shape[1]
    gradient = came_ref[0].astype(jnp.float32)
    for k in range(1, 4):
        gradient += came_ref[k].astype(jnp.float32)
    out_ref[0, :, :early] = step_ref[...]
    out_ref[0, :, early:] = update(gradient, first_ref[0, :, early:], second_ref[0, :, early:])


def body(grad_out, hidden, expert_ids, route_weights, first_moment, second_moment):
    chips = lax.axis_size("z")
    width, features = hidden.shape[2], grad_out.shape[1]
    early = features - LATE
    where = jnp.stack([lax.axis_index(a) for a in ("z", "core", "opt", "rep")]).astype(jnp.int32)
    grad_p = turn(grad_out, "core", 1)
    tokens = hidden.shape[0]
    pack = call(
        pack_kernel,
        jax.ShapeDtypeStruct((2, tokens + 16, width), jnp.bfloat16),
        [pl.BlockSpec()] * 3,
        expert_ids.T, route_weights.T, hidden,
    )
    bf16 = jnp.bfloat16

    def blocks(n, columns):
        return jax.ShapeDtypeStruct((n, PAIR, columns), bf16)

    outs = [blocks(chips, features - early)] + [blocks(len(s), width + early) for s in SHORT_SENDS]
    outs += [blocks(len(LONG) + 1, width + early)]
    second, *short, rest = pl.pallas_call(
        functools.partial(fill_kernel, chips),
        out_shape=outs,
        in_specs=[SMEM] + [VMEM] * 4,
        out_specs=[VMEM] * len(outs),
        scratch_shapes=[pltpu.VMEM((chips, PAIR, width + early), bf16)],
        compiler_params=PARAMS,
    )(where, grad_out, grad_p, pack, turn(pack, "core", 1))
    short = [turn(x, "z", d) for x, d in zip(short, SHORT)]
    far = call(
        join_kernel,
        [blocks(len(s), width + early) for s in LONG_SENDS],
        [VMEM] * (1 + len(short)),
        rest, *short,
    )
    far = [turn(x, "z", d) for x, d in zip(far, LONG)]
    second = lax.all_to_all(second, "z", split_axis=0, concat_axis=0, tiled=True)
    units, first = call(
        functools.partial(gather_kernel, chips),
        [blocks(chips, width), blocks(chips, early)],
        [SMEM] + [VMEM] * (1 + len(short) + len(far)),
        where, rest, *short, *far,
        cost=pl.CostEstimate(flops=2000000000000, bytes_accessed=0, transcendentals=0),
    )
    units = [units, turn(units, "opt", 1), turn(units, "opt", -1), turn(units, "opt", 2)]
    shape = (width, chips * PAIR)
    kept, *sent, units = call(
        first_kernel,
        [jax.ShapeDtypeStruct((width, early), bf16)] * 4 + [jax.ShapeDtypeStruct((4,) + shape, bf16)],
        [SMEM] + [VMEM] * 5,
        where, *units, first,
    )
    came = [turn(part, "rep", k + 1) for k, part in enumerate(sent)]
    gradient = sum((part.astype(jnp.float32) for part in came), kept.astype(jnp.float32))
    step = update(gradient, first_moment[0, :, :early], second_moment[0, :, :early])
    sent = call(
        second_kernel,
        jax.ShapeDtypeStruct((4, width, features - early), bf16),
        [VMEM] * 2 + [ANY] * len(came),
        units, second, *came,
    )
    came = lax.all_to_all(sent, "rep", split_axis=0, concat_axis=0, tiled=True)
    return call(
        finish_kernel,
        jax.ShapeDtypeStruct(first_moment.shape, bf16),
        [VMEM] * 4,
        step, came, first_moment, second_moment,
    )


def solution(mesh):
    reps, exps, opts = (mesh.shape[a] for a in ("rep", "exp", "opt"))
    split = Mesh(mesh.devices.reshape(reps, exps // 2, 2, opts), ("rep", "z", "core", "opt"))
    exp = ("z", "core")
    tokens = ("rep",) + exp
    placed = (
        P(tokens, "opt"),
        P(tokens, None, "opt"),
        P(tokens, None),
        P(tokens, None),
        P(exp, "rep", "opt"),
        P(exp, "rep", "opt"),
    )
    return jax.shard_map(
        body, mesh=split, in_specs=placed, out_specs=P(exp, "rep", "opt"), check_vma=False
    )
```
